32 devices in a mesh: groups: 2 (over y), pool: 4 (over z), head: 2 (over x), rep: 2 (over core).
Axes of the slice: x: 2, y: 2, z: 4, core: 2. Of those that a mesh axis runs over, the one named last changes fastest.
Arguments:
- queries: bfloat16 [2048, 4096], P(('groups', 'pool'), ('head', 'rep')), parts along dimension 0, may hold values from -200 to 200
- token_key_value: bfloat16 [2048, 1024], P(('groups', 'pool'), 'head'), parts along dimension 0, may hold values from -6 to 6
- key_value_cache: bfloat16 [96, 16, 1024], P(('groups', 'pool'), None, 'head'), parts along dimension 0, may hold values from -6 to 6
- cached_block_slots: int32 [24], P('groups'), parts along dimension 0, may hold values from 0 to 47, as said below
- absent_hidden_rows: bfloat16 [256, 8192], P(('groups', 'pool'), 'rep'), parts along dimension 0, may hold values from -6 to 6
- absent_block_count: int32 [8], P('groups'), parts along dimension 0, may hold values from 1 to 2, as said below
- adapter: int32 [2], P('groups'), parts along dimension 0, may hold values from 0 to 7
- key_value_weight: bfloat16 [8192, 1024], P('rep', 'head'), may hold values from -0.0625 to 0.0625
- down_weight_stack: bfloat16 [8, 16, 8192], P(None, None, 'rep'), may hold values from -0.0625 to 0.0625
- up_weight_stack: bfloat16 [8, 16, 1024], P(None, None, 'head'), may hold values from -0.75 to 0.75
Outputs:
- attended: bfloat16 [2048, 4096], P(('groups', 'pool'), ('head', 'rep')), parts along dimension 0
- rebuilt_key_value: bfloat16 [256, 1024], P(('groups', 'pool'), 'head'), parts along dimension 0
The draws below stay inside these ranges and needn't reach their ends.
There are 2 independent parts, one for each index of `groups`. The reference program is written for one: setup_inputs(seed, part) draws one part's arguments, and reference() takes and returns one part's arrays. A program takes and returns all parts, laid end to end along the dimension named above; an argument that names none is the same for every part. Nothing has to cross between parts.
Inputs may be any that keep to these rules, and one draw needn't show every extreme that they name: `cached_block_slots`: entries are distinct cache slot numbers; slot s lies on pool device s // 12; no pool device holds more than 9 of the entries, and one holds exactly 9. `absent_block_count`: some pool device holds exactly 2 missing blocks.
All inputs are finite; a program needn't handle non-finite values.
Results may differ from the reference program's by a relative error of at most 0.011.
Values may be sent and summed in bfloat16 or wider, within the bound.
A program may use at most 64 MiB of HBM per device.

```python
import math
import jax
import jax.numpy as jnp
from jax import lax

MODEL_WIDTH = 8192
HEAD_WIDTH = 128
KEY_VALUE_HEADS = 4
KV_GROUP = 8
ADAPTER_RANK = 16
ADAPTER_COUNT = 8
BLOCK = 16
MISS_DEV = 2
TOKENS = 1024
HITS = 12
OWNER_MOST = 9
SLOTS = 12
N_POOL = 4


def span_base(key):
    base_kv = jnp.clip(jax.random.normal(key, (TOKENS, KEY_VALUE_HEADS, 2, HEAD_WIDTH), jnp.float32), -6.0, 6.0)
    return base_kv


def slot_list(key):
    key = jax.random.fold_in(key, 7)
    busy_owner = jax.random.randint(jax.random.fold_in(key, 1), (), 0, N_POOL)
    picked_ids = jax.random.permutation(jax.random.fold_in(key, 2), (N_POOL - 1) * OWNER_MOST)[:HITS - OWNER_MOST]
    other_owner = picked_ids // OWNER_MOST
    other_owner = other_owner + (other_owner >= busy_owner).astype(other_owner.dtype)
    owner_ids = jnp.concatenate([jnp.full((OWNER_MOST,), busy_owner, dtype=other_owner.dtype), other_owner])
    owner_rank = jnp.concatenate([jnp.arange(OWNER_MOST, dtype=other_owner.dtype), picked_ids % OWNER_MOST])
    rotation = jax.random.randint(jax.random.fold_in(key, 3), (N_POOL,), 0, SLOTS)
    slot_ids = (owner_rank + rotation[owner_ids]) % SLOTS
    global_ids = owner_ids * SLOTS + slot_ids
    shuffle_order = jax.random.permutation(jax.random.fold_in(key, 4), HITS)
    return global_ids[shuffle_order].astype(jnp.int32)


def aim_targets(key):
    slots = slot_list(key)
    inner = jax.random.fold_in(key, 31)
    pick = jax.random.randint(jax.random.fold_in(inner, 1), (TOKENS,), 0, HITS)
    target_row = jax.random.randint(jax.random.fold_in(inner, 2), (TOKENS,), 0, BLOCK)
    target_strength = jax.random.uniform(jax.random.fold_in(inner, 3), (TOKENS,), jnp.float32, 20.0, 35.0)
    aimed = jnp.arange(TOKENS) % 64 == 31
    return (slots[pick], target_row, target_strength, aimed)


def cache_base(key):
    target_slot, target_row, target_strength, aimed = aim_targets(key)
    inner = jax.random.fold_in(key, 41)
    slot_total = N_POOL * SLOTS
    base = jnp.clip(jax.random.normal(inner, (slot_total, BLOCK, KEY_VALUE_HEADS, 2, HEAD_WIDTH), jnp.float32), -6.0, 6.0)
    faint = jax.random.randint(jax.random.fold_in(inner, 1), (slot_total, BLOCK), 0, 4) == 0
    marked = jnp.zeros((slot_total, BLOCK), jnp.int32).at[target_slot, target_row].max(aimed.astype(jnp.int32))
    faint = faint | (marked > 0)
    factor = jnp.where(faint, 0.5, 1.0).astype(jnp.float32)
    key_part = base[:, :, :, 0, :] * factor[:, :, None, None]
    return jnp.stack([key_part, base[:, :, :, 1, :]], axis=3)


def draw_token_key_value(key, part):
    base_kv = span_base(key)
    return base_kv.reshape(TOKENS, KEY_VALUE_HEADS * 2 * HEAD_WIDTH).astype(jnp.bfloat16)


def draw_key_value_cache(key, part):
    cache_rows = cache_base(key)
    return cache_rows.reshape(N_POOL * SLOTS, BLOCK, KEY_VALUE_HEADS * 2 * HEAD_WIDTH).astype(jnp.bfloat16)


def draw_queries(key, part):
    cache_rows = cache_base(key)
    target_slot, target_row, target_strength, aimed = aim_targets(key)
    key = jax.random.fold_in(key, 22)
    head_count = KEY_VALUE_HEADS * KV_GROUP
    row_scale = jnp.exp(jax.random.uniform(jax.random.fold_in(key, 5), (TOKENS, head_count, 1), jnp.float32, math.log(1.5), math.log(18.0)))
    base_draw = jnp.clip(jax.random.normal(key, (TOKENS, head_count, HEAD_WIDTH), jnp.float32), -6.0, 6.0) * row_scale
    target_keys = cache_rows[target_slot, target_row, :, 0, :]
    aimed_rows = jnp.repeat(target_keys, KV_GROUP, axis=1) * target_strength[:, None, None]
    base_draw = jnp.where(aimed[:, None, None], aimed_rows, base_draw)
    base_draw = jnp.clip(base_draw, -200.0, 200.0)
    return base_draw.reshape(TOKENS, head_count * HEAD_WIDTH).astype(jnp.bfloat16)


def draw_cached_block_slots(key, part):
    return slot_list(key)


def draw_absent_block_count(key, part):
    key = jax.random.fold_in(key, 9)
    counts = jax.random.randint(jax.random.fold_in(key, 1), (N_POOL,), 1, MISS_DEV + 1)
    full_owner = jax.random.randint(jax.random.fold_in(key, 2), (), 0, N_POOL)
    return jnp.where(jnp.arange(N_POOL) == full_owner, MISS_DEV, counts).astype(jnp.int32)


def block_scale(stream_key, dims, shards, smallest, high):
    def one(dim, blocks):
        steps = jax.random.uniform(jax.random.fold_in(jax.random.fold_in(stream_key, 6), dim), (blocks,), jnp.float32, smallest / len(shards), high / len(shards))
        return jnp.repeat(jnp.exp(steps), dims[dim] // blocks).reshape((-1,) + (1,) * (len(dims) - dim - 1))

    factor_of = one(*shards[0])
    for cut in shards[1:]:
        factor_of = factor_of * one(*cut)
    return factor_of


def bell_draw(stream_key, dims, spread, bound, shards=(), kind=jnp.bfloat16):
    result = jax.random.normal(stream_key, dims, jnp.float32) * spread
    if len(shards) > 0:
        result = block_scale(stream_key, dims, shards, -0.22, 0.18) * result
    return jnp.clip(result, min=-bound, max=bound).astype(kind)


def setup_inputs(seed: int = 0, part: int = 0) -> dict:
    keys = jax.random.split(jax.random.key(seed), 11)
    part_keys = jax.random.split(jax.random.fold_in(keys[10], part), 11)
    queries = draw_queries(jax.random.fold_in(jax.random.fold_in(keys[10], part), 71), part)
    token_key_value = draw_token_key_value(jax.random.fold_in(jax.random.fold_in(keys[10], part), 71), part)
    key_value_cache = draw_key_value_cache(jax.random.fold_in(jax.random.fold_in(keys[10], part), 71), part)
    cached_block_slots = draw_cached_block_slots(jax.random.fold_in(jax.random.fold_in(keys[10], part), 71), part)
    absent_hidden_rows = bell_draw(part_keys[4], (N_POOL * MISS_DEV * BLOCK, MODEL_WIDTH), 1.0, 6.0, ((0, 4), (1, 2)))
    absent_block_count = draw_absent_block_count(jax.random.fold_in(jax.random.fold_in(keys[10], part), 71), part)
    adapter = jax.random.randint(part_keys[6], (1,), 0, ADAPTER_COUNT).astype(jnp.int32)
    key_value_weight = bell_draw(keys[7], (MODEL_WIDTH, KEY_VALUE_HEADS * 2 * HEAD_WIDTH), MODEL_WIDTH ** -0.5, 0.0625, ((0, 2), (1, 2)))
    down_weight_stack = bell_draw(keys[8], (ADAPTER_COUNT, ADAPTER_RANK, MODEL_WIDTH), MODEL_WIDTH ** -0.5, 0.0625, ((2, 2),))
    up_weight_stack = bell_draw(keys[9], (ADAPTER_COUNT, ADAPTER_RANK, KEY_VALUE_HEADS * 2 * HEAD_WIDTH), (4 * ADAPTER_RANK) ** -0.5, 0.75, ((2, 2),))
    return dict(queries=queries, token_key_value=token_key_value, key_value_cache=key_value_cache, cached_block_slots=cached_block_slots, absent_hidden_rows=absent_hidden_rows, absent_block_count=absent_block_count, adapter=adapter, key_value_weight=key_value_weight, down_weight_stack=down_weight_stack, up_weight_stack=up_weight_stack)


ADAPTER_SCALE = 2.0
NEG_BIG = -1.0e30


def rebuild_blocks(absent_hidden_rows, absent_block_count, adapter, key_value_weight, down_weight_stack, up_weight_stack):
    picked_down_weight = lax.dynamic_index_in_dim(down_weight_stack, adapter[0], 0, keepdims=False)
    picked_up_weight = lax.dynamic_index_in_dim(up_weight_stack, adapter[0], 0, keepdims=False)
    plain_projection = jnp.dot(absent_hidden_rows, key_value_weight, preferred_element_type=jnp.float32)
    adapter_delta = jnp.einsum("nd,rd->nr", absent_hidden_rows.astype(jnp.float32), picked_down_weight.astype(jnp.float32), precision=lax.Precision.HIGHEST)
    reduced_total = plain_projection + ADAPTER_SCALE * jnp.dot(adapter_delta, picked_up_weight.astype(jnp.float32), precision=lax.Precision.HIGHEST)
    block_ids = jnp.arange(absent_hidden_rows.shape[0]) // BLOCK
    present_rows = (block_ids % MISS_DEV) < absent_block_count[block_ids // MISS_DEV]
    return jnp.where(present_rows[:, None], reduced_total, jnp.float32(0.0)).astype(jnp.bfloat16), present_rows


def reference(queries, token_key_value, key_value_cache, cached_block_slots, absent_hidden_rows, absent_block_count, adapter, key_value_weight, down_weight_stack, up_weight_stack):
    rebuilt_key_value, present_rows = rebuild_blocks(absent_hidden_rows, absent_block_count, adapter, key_value_weight, down_weight_stack, up_weight_stack)
    kv_cols = token_key_value.shape[1]
    hit_rows = key_value_cache[cached_block_slots].reshape(HITS * BLOCK, kv_cols)
    prefix_kv = jnp.concatenate([hit_rows, rebuilt_key_value], axis=0)
    prefix_ok = jnp.concatenate([jnp.ones((HITS * BLOCK,), dtype=jnp.bool_), present_rows])
    scale = HEAD_WIDTH ** -0.5
    row_block = min(512, TOKENS)
    pieces = []
    for start in range(0, TOKENS, row_block):
        stop = start + row_block
        keys_all = jnp.concatenate([prefix_kv, token_key_value[:stop]], axis=0).reshape(-1, KEY_VALUE_HEADS, 2, HEAD_WIDTH)
        causal = jnp.arange(stop)[None, :] <= jnp.arange(start, stop)[:, None]
        allowed = jnp.concatenate([jnp.broadcast_to(prefix_ok[None, :], (row_block, prefix_ok.shape[0])), causal], axis=1)
        query_block = queries[start:stop].reshape(row_block, KEY_VALUE_HEADS, KV_GROUP, HEAD_WIDTH).astype(jnp.float32)
        heads_out = []
        for group in range(KEY_VALUE_HEADS):
            key_rows = keys_all[:, group, 0, :].astype(jnp.float32)
            value_rows = keys_all[:, group, 1, :].astype(jnp.float32)
            scores = jnp.einsum("tqd,kd->qtk", query_block[:, group], key_rows, precision=lax.Precision.HIGHEST) * scale
            scores = jnp.where(allowed[None], scores, NEG_BIG)
            highest = jnp.max(scores, axis=-1, keepdims=True)
            weights = jnp.where(allowed[None], jnp.exp(scores - highest), jnp.float32(0.0))
            totals = jnp.sum(weights, axis=-1)
            rounded = lax.optimization_barrier(weights.astype(jnp.bfloat16)).astype(jnp.float32)
            mixed = jnp.einsum("qtk,kd->tqd", rounded, value_rows, precision=lax.Precision.HIGHEST)
            heads_out.append(mixed / jnp.transpose(totals)[:, :, None])
        pieces.append(jnp.stack(heads_out, axis=1).reshape(row_block, KEY_VALUE_HEADS * KV_GROUP * HEAD_WIDTH))
    attended = jnp.concatenate(pieces, axis=0).astype(jnp.bfloat16)
    return attended, rebuilt_key_value
```

```python
import functools
import math

import jax
import jax.numpy as jnp
from jax import lax
from jax.experimental import pallas as pl
from jax.experimental.pallas import tpu as pltpu
from jax.sharding import PartitionSpec as P

HEAD_WIDTH = 128
KV_WIDTH = 2 * HEAD_WIDTH
KV_GROUP = 8
BLOCK = 16
OWNER_MOST = 9
ADAPTER_SCALE = 2.0
NEG_BIG = -1e30
MESH = pl.DeviceIdType.MESH
SCORE_SCALE = HEAD_WIDTH ** -0.5 * math.log2(math.e)
WEIGHT_CUTS = 4


def kernel(
    pool_size,
    slots_ref,
    count_ref,
    adapter_ref,
    query_hbm,
    token_hbm,
    cache_hbm,
    hidden_hbm,
    weight_hbm,
    down_hbm,
    up_hbm,
    out_ref,
    rebuilt_ref,
    query_ref,
    token_all,
    cache_ref,
    hidden_ref,
    weight_ref,
    down_ref,
    up_ref,
    hit_all,
    miss_all,
    part_send,
    part_recv,
    extra_kv,
    top_ref,
    acc_ref,
    local_sem,
    weight_sem,
    token_send,
    token_recv,
    hit_send,
    hit_recv,
    miss_send,
    miss_recv,
    part_sem,
):
    me = lax.axis_index("pool")
    core = lax.axis_index("rep")
    partner = 1 - core
    hits = slots_ref.shape[0]
    slot_count = cache_ref.shape[0]
    rows = query_ref.shape[0]
    heads = query_ref.shape[1] // HEAD_WIDTH
    first_head = core * heads // KV_GROUP
    columns = pl.ds(pl.multiple_of(first_head * KV_WIDTH, KV_WIDTH), KV_WIDTH)
    miss_rows = hidden_ref.shape[0]
    miss_slots = miss_rows // BLOCK

    barrier = pltpu.get_barrier_semaphore()
    for step in range(1, pool_size):
        pl.semaphore_signal(
            barrier, inc=1, device_id={"pool": lax.rem(me + step, pool_size)}, device_id_type=MESH
        )
    pl.semaphore_signal(barrier, inc=1, device_id={"rep": partner}, device_id_type=MESH)

    token_in = pltpu.make_async_copy(token_hbm.at[:, columns], token_all.at[me], local_sem.at[0])
    cache_in = pltpu.make_async_copy(cache_hbm.at[:, :, columns], cache_ref, local_sem.at[1])
    query_in = pltpu.make_async_copy(query_hbm, query_ref, local_sem.at[2])
    hidden_in = pltpu.make_async_copy(hidden_hbm, hidden_ref, local_sem.at[3])
    down_in = pltpu.make_async_copy(down_hbm, down_ref, local_sem.at[4])
    up_in = pltpu.make_async_copy(up_hbm, up_ref, local_sem.at[5])
    token_in.start()
    cache_in.start()
    query_in.start()
    hidden_in.start()
    depth = weight_ref.shape[0] // WEIGHT_CUTS
    weight_in = []
    for cut in range(WEIGHT_CUTS):
        span = pl.ds(cut * depth, depth)
        copy = pltpu.make_async_copy(weight_hbm.at[span], weight_ref.at[span], weight_sem.at[cut])
        copy.start()
        weight_in.append(copy)
    down_in.start()
    up_in.start()

    slot_ids = [slots_ref[i] for i in range(hits)]
    owners = [slot // slot_count for slot in slot_ids]
    ranks = []
    for i in range(hits):
        rank = jnp.int32(0)
        for j in range(i):
            rank = rank + (owners[j] == owners[i]).astype(jnp.int32)
        ranks.append(rank)
    place = [jnp.where(owners[i] == me, ranks[i], -1) for i in range(hits)]

    cache_in.wait()
    for j in range(OWNER_MOST):
        local_slot = jnp.int32(0)
        for i in range(hits):
            local_slot = jnp.where(place[i] == j, lax.rem(slot_ids[i], slot_count), local_slot)
        hit_all[me, j] = cache_ref[local_slot]
    token_in.wait()

    def remote(buffer, source, target, send, receive):
        return pltpu.make_async_remote_copy(
            src_ref=buffer.at[source],
            dst_ref=buffer.at[source],
            send_sem=send.at[target],
            recv_sem=receive.at[source],
            device_id={"pool": target},
            device_id_type=MESH,
        )

    pl.semaphore_wait(barrier, pool_size)
    for step in range(1, pool_size):

        @pl.when(me + step < pool_size)
        def _():
            remote(token_all, me, me + step, token_send, token_recv).start()

    for step in range(1, pool_size):
        target = lax.rem(me + step, pool_size)
        remote(hit_all, me, target, hit_send, hit_recv).start()

    def scores_of(head, keys):
        query = query_ref[:, head * HEAD_WIDTH : (head + 1) * HEAD_WIDTH]
        return (
            lax.dot_general(
                query, keys, (((1,), (1,)), ((), ())), preferred_element_type=jnp.float32
            )
            * SCORE_SCALE
        )

    def values_of(kv):
        return jnp.concatenate(
            [kv[:, HEAD_WIDTH:], jnp.ones((kv.shape[0], HEAD_WIDTH), kv.dtype)], axis=1
        )

    def first_attend(head_list):
        kv = token_all[me]
        keys, values = kv[:, :HEAD_WIDTH], values_of(kv)
        row_ids = lax.broadcasted_iota(jnp.int32, (rows, rows), 0)
        column_ids = lax.broadcasted_iota(jnp.int32, (rows, rows), 1)
        allowed = column_ids <= row_ids
        for head in head_list:
            score = jnp.where(allowed, scores_of(head, keys), NEG_BIG)
            top = jnp.max(score, axis=1, keepdims=True)
            weights = jnp.exp2(score - top).astype(jnp.bfloat16)
            top_ref[head] = jnp.broadcast_to(top, (rows, HEAD_WIDTH))
            acc_ref[head] = jnp.dot(weights, values, preferred_element_type=jnp.float32)

    def attend(kv, allowed, last):
        keys, values = kv[:, :HEAD_WIDTH], values_of(kv)
        for head in range(heads):
            score = scores_of(head, keys)
            if allowed is not None:
                score = jnp.where(allowed, score, NEG_BIG)
            old = top_ref[head][:, :1]
            top = jnp.maximum(old, jnp.max(score, axis=1, keepdims=True))
            weights = jnp.exp2(score - top).astype(jnp.bfloat16)
            total = acc_ref[head] * jnp.exp2(old - top) + jnp.dot(
                weights, values, preferred_element_type=jnp.float32
            )
            if last:
                out_ref[:, head * HEAD_WIDTH : (head + 1) * HEAD_WIDTH] = (
                    total[:, :HEAD_WIDTH] / total[:, HEAD_WIDTH:]
                ).astype(out_ref.dtype)
            else:
                top_ref[head] = jnp.broadcast_to(top, (rows, HEAD_WIDTH))
                acc_ref[head] = total

    query_in.wait()
    first_attend(range(heads // 2))

    hidden_in.wait()
    partial = None
    for cut in range(WEIGHT_CUTS):
        weight_in[cut].wait()
        span = slice(cut * depth, (cut + 1) * depth)
        product = jnp.dot(
            hidden_ref[:, span], weight_ref[span, :], preferred_element_type=jnp.float32
        )
        partial = product if partial is None else partial + product
    down_in.wait()
    up_in.wait()
    adapters, rank_width, width = down_ref.shape
    delta = lax.dot_general(
        hidden_ref[...],
        down_ref[...].reshape(adapters * rank_width, width),
        (((1,), (1,)), ((), ())),
        preferred_element_type=jnp.float32,
    )
    adapter_of = lax.broadcasted_iota(jnp.int32, delta.shape, 1) // rank_width
    delta = jnp.where(adapter_of == adapter_ref[0], delta, 0.0)
    up_all = up_ref[...].reshape(adapters * rank_width, up_ref.shape[2]).astype(jnp.float32)
    part_send[...] = partial + ADAPTER_SCALE * jnp.dot(
        delta, up_all, preferred_element_type=jnp.float32, precision=lax.Precision.HIGHEST
    )
    part_copy = pltpu.make_async_remote_copy(
        src_ref=part_send,
        dst_ref=part_recv,
        send_sem=part_sem.at[0],
        recv_sem=part_sem.at[1],
        device_id={"rep": partner},
        device_id_type=MESH,
    )
    part_copy.start()

    first_attend(range(heads // 2, heads))

    part_copy.wait_recv()
    present = lax.broadcasted_iota(jnp.int32, part_send.shape, 0) // BLOCK < count_ref[me]
    rebuilt_ref[...] = jnp.where(present, part_send[...] + part_recv[...], 0.0).astype(
        jnp.bfloat16
    )
    miss_all[me] = rebuilt_ref[:, columns]
    for step in range(1, pool_size):
        target = lax.rem(me + step, pool_size)
        remote(miss_all, me, target, miss_send, miss_recv).start()

    def earlier(step, carry):
        source = me - 1 - step
        remote(token_all, source, source, token_send, token_recv).wait_recv()
        attend(token_all[source], None, False)
        return carry

    lax.fori_loop(0, me, earlier, 0)

    for step in range(1, pool_size):
        source = lax.rem(me + step, pool_size)
        remote(hit_all, source, source, hit_send, hit_recv).wait_recv()
    for i in range(hits):
        extra_kv[i * BLOCK : (i + 1) * BLOCK, :] = hit_all[
            jnp.clip(owners[i], 0, pool_size - 1), jnp.minimum(ranks[i], OWNER_MOST - 1)
        ]
    for step in range(1, pool_size):
        source = lax.rem(me + step, pool_size)
        remote(miss_all, source, source, miss_send, miss_recv).wait_recv()
    for holder in range(pool_size):
        start = hits * BLOCK + holder * miss_rows
        extra_kv[start : start + miss_rows, :] = miss_all[holder]

    extra_rows = extra_kv.shape[0]
    ids = lax.broadcasted_iota(jnp.int32, (1, extra_rows), 1) - hits * BLOCK
    live = jnp.where(ids < 0, 1, 0)
    for holder in range(pool_size):
        offset = ids - holder * miss_rows
        limit = jnp.minimum(count_ref[holder], miss_slots) * BLOCK
        live = live + jnp.where((offset >= 0) & (offset < limit), 1, 0)
    attend(extra_kv[...], live > 0, True)

    for step in range(1, pool_size):

        @pl.when(me + step < pool_size)
        def _():
            remote(token_all, me, me + step, token_send, token_recv).wait_send()

    for step in range(1, pool_size):
        target = lax.rem(me + step, pool_size)
        remote(hit_all, me, target, hit_send, hit_recv).wait_send()
        remote(miss_all, me, target, miss_send, miss_recv).wait_send()
    part_copy.wait_send()


def shards(
    queries,
    token_key_value,
    key_value_cache,
    cached_block_slots,
    absent_hidden_rows,
    absent_block_count,
    adapter,
    key_value_weight,
    down_weight_stack,
    up_weight_stack,
):
    pool_size = lax.axis_size("pool")
    rows, query_width = queries.shape
    heads = query_width // HEAD_WIDTH
    slot_count = key_value_cache.shape[0]
    hits = cached_block_slots.shape[0]
    miss_rows = absent_hidden_rows.shape[0]
    kv_columns = token_key_value.shape[1]
    extra_rows = hits * BLOCK + pool_size * miss_rows
    smem = pl.BlockSpec(memory_space=pltpu.SMEM)
    anywhere = pl.BlockSpec(memory_space=pl.ANY)
    vmem = pl.BlockSpec(memory_space=pltpu.VMEM)
    dma = pltpu.SemaphoreType.DMA
    bf16 = jnp.bfloat16
    return pl.pallas_call(
        functools.partial(kernel, pool_size),
        out_shape=(
            jax.ShapeDtypeStruct((rows, query_width), bf16),
            jax.ShapeDtypeStruct((miss_rows, kv_columns), bf16),
        ),
        in_specs=[smem] * 3 + [anywhere] * 7,
        out_specs=(vmem, vmem),
        scratch_shapes=[
            pltpu.VMEM((rows, query_width), bf16),
            pltpu.VMEM((pool_size, rows, KV_WIDTH), bf16),
            pltpu.VMEM((slot_count, BLOCK, KV_WIDTH), bf16),
            pltpu.VMEM(absent_hidden_rows.shape, bf16),
            pltpu.VMEM(key_value_weight.shape, bf16),
            pltpu.VMEM(down_weight_stack.shape, bf16),
            pltpu.VMEM(up_weight_stack.shape, bf16),
            pltpu.VMEM((pool_size, OWNER_MOST, BLOCK, KV_WIDTH), bf16),
            pltpu.VMEM((pool_size, miss_rows, KV_WIDTH), bf16),
            pltpu.VMEM((miss_rows, kv_columns), jnp.float32),
            pltpu.VMEM((miss_rows, kv_columns), jnp.float32),
            pltpu.VMEM((extra_rows, KV_WIDTH), bf16),
            pltpu.VMEM((heads, rows, HEAD_WIDTH), jnp.float32),
            pltpu.VMEM((heads, rows, KV_WIDTH), jnp.float32),
            dma((6,)),
            dma((WEIGHT_CUTS,)),
            dma((pool_size,)),
            dma((pool_size,)),
            dma((pool_size,)),
            dma((pool_size,)),
            dma((pool_size,)),
            dma((pool_size,)),
            dma((2,)),
        ],
        compiler_params=pltpu.CompilerParams(
            collective_id=0, has_side_effects=True, vmem_limit_bytes=48 * 1024 * 1024
        ),
        cost_estimate=pl.CostEstimate(
            flops=4 * heads * rows * HEAD_WIDTH * (pool_size * rows + extra_rows),
            bytes_accessed=key_value_weight.size * 2,
            transcendentals=heads * rows * (pool_size * rows + extra_rows),
        ),
    )(
        cached_block_slots,
        absent_block_count,
        adapter,
        queries,
        token_key_value,
        key_value_cache,
        absent_hidden_rows,
        key_value_weight,
        down_weight_stack,
        up_weight_stack,
    )


def solution(mesh):
    in_specs = (
        P(("groups", "pool"), ("head", "rep")),
        P(("groups", "pool"), "head"),
        P(("groups", "pool"), None, "head"),
        P("groups"),
        P(("groups", "pool"), "rep"),
        P("groups"),
        P("groups"),
        P("rep", "head"),
        P(None, None, "rep"),
        P(None, None, "head"),
    )
    out_specs = (P(("groups", "pool"), ("head", "rep")), P(("groups", "pool"), "head"))
    return jax.shard_map(shards, mesh=mesh, in_specs=in_specs, out_specs=out_specs, check_vma=False)
```

```python
import functools
import math

import jax
import jax.numpy as jnp
from jax import lax
from jax.experimental import pallas as pl
from jax.experimental.pallas import tpu as pltpu
from jax.sharding import PartitionSpec as P

HEAD_WIDTH = 128
KV_WIDTH = 2 * HEAD_WIDTH
KV_GROUP = 8
BLOCK = 16
OWNER_MOST = 9
ADAPTER_SCALE = 2.0
NEG_BIG = -1e30
MESH = pl.DeviceIdType.MESH
SCORE_SCALE = HEAD_WIDTH ** -0.5 * math.log2(math.e)
WEIGHT_CUTS = 4


def kernel(
    pool_size,
    slots_ref,
    count_ref,
    adapter_ref,
    query_hbm,
    token_hbm,
    cache_hbm,
    hidden_hbm,
    weight_hbm,
    down_hbm,
    up_hbm,
    out_ref,
    rebuilt_ref,
    query_ref,
    token_all,
    cache_ref,
    hidden_ref,
    weight_ref,
    down_ref,
    up_ref,
    hit_all,
    miss_all,
    part_send,
    part_recv,
    extra_kv,
    top_ref,
    acc_ref,
    local_sem,
    weight_sem,
    token_send,
    token_recv,
    hit_send,
    hit_recv,
    miss_send,
    miss_recv,
    part_sem,
):
    me = lax.axis_index("pool")
    core = lax.axis_index("rep")
    partner = 1 - core
    hits = slots_ref.shape[0]
    slot_count = cache_ref.shape[0]
    rows = query_ref.shape[0]
    heads = query_ref.shape[1] // HEAD_WIDTH
    first_head = core * heads // KV_GROUP
    columns = pl.ds(pl.multiple_of(first_head * KV_WIDTH, KV_WIDTH), KV_WIDTH)
    miss_rows = hidden_ref.shape[0]
    miss_slots = miss_rows // BLOCK

    barrier = pltpu.get_barrier_semaphore()
    for step in range(1, pool_size):
        pl.semaphore_signal(
            barrier, inc=1, device_id={"pool": lax.rem(me + step, pool_size)}, device_id_type=MESH
        )
    pl.semaphore_signal(barrier, inc=1, device_id={"rep": partner}, device_id_type=MESH)

    token_in = pltpu.make_async_copy(token_hbm.at[:, columns], token_all.at[me], local_sem.at[0])
    cache_in = pltpu.make_async_copy(cache_hbm.at[:, :, columns], cache_ref, local_sem.at[1])
    query_in = pltpu.make_async_copy(query_hbm, query_ref, local_sem.at[2])
    hidden_in = pltpu.make_async_copy(hidden_hbm, hidden_ref, local_sem.at[3])
    down_in = pltpu.make_async_copy(down_hbm, down_ref, local_sem.at[4])
    up_in = pltpu.make_async_copy(up_hbm, up_ref, local_sem.at[5])
    token_in.start()
    cache_in.start()
    query_in.start()
    hidden_in.start()
    depth = weight_ref.shape[0] // WEIGHT_CUTS
    weight_in = []
    for cut in range(WEIGHT_CUTS):
        span = pl.ds(cut * depth, depth)
        copy = pltpu.make_async_copy(weight_hbm.at[span], weight_ref.at[span], weight_sem.at[cut])
        copy.start()
        weight_in.append(copy)
    down_in.start()
    up_in.start()

    slot_ids = [slots_ref[i] for i in range(hits)]
    owners = [slot // slot_count for slot in slot_ids]
    ranks = []
    for i in range(hits):
        rank = jnp.int32(0)
        for j in range(i):
            rank = rank + (owners[j] == owners[i]).astype(jnp.int32)
        ranks.append(rank)
    place = [jnp.where(owners[i] == me, ranks[i], -1) for i in range(hits)]

    cache_in.wait()
    for j in range(OWNER_MOST):
        local_slot = jnp.int32(0)
        for i in range(hits):
            local_slot = jnp.where(place[i] == j, lax.rem(slot_ids[i], slot_count), local_slot)
        hit_all[me, j] = cache_ref[local_slot]
    token_in.wait()

    def remote(buffer, source, target, send, receive):
        return pltpu.make_async_remote_copy(
            src_ref=buffer.at[source],
            dst_ref=buffer.at[source],
            send_sem=send.at[target],
            recv_sem=receive.at[source],
            device_id={"pool": target},
            device_id_type=MESH,
        )

    pl.semaphore_wait(barrier, pool_size)

    def token_copy(source):
        return pltpu.make_async_remote_copy(
            src_ref=token_all.at[source],
            dst_ref=token_all.at[source],
            send_sem=token_send.at[source],
            recv_sem=token_recv.at[source],
            device_id={"pool": lax.rem(me + 1, pool_size)},
            device_id_type=MESH,
        )

    def take_token(step):
        token_copy(me - 1 - step).wait_recv()

        @pl.when(me + 1 < pool_size)
        def _():
            token_copy(me - 1 - step).start()

    @pl.when(me + 1 < pool_size)
    def _():
        token_copy(me).start()

    for step in range(1, pool_size):
        target = lax.rem(me + step, pool_size)
        remote(hit_all, me, target, hit_send, hit_recv).start()

    def scores_of(head, keys):
        query = query_ref[:, head * HEAD_WIDTH : (head + 1) * HEAD_WIDTH]
        return (
            lax.dot_general(
                query, keys, (((1,), (1,)), ((), ())), preferred_element_type=jnp.float32
            )
            * SCORE_SCALE
        )

    def values_of(kv):
        return jnp.concatenate(
            [kv[:, HEAD_WIDTH:], jnp.ones((kv.shape[0], HEAD_WIDTH), kv.dtype)], axis=1
        )

    def first_attend(head_list):
        kv = token_all[me]
        keys, values = kv[:, :HEAD_WIDTH], values_of(kv)
        row_ids = lax.broadcasted_iota(jnp.int32, (rows, rows), 0)
        column_ids = lax.broadcasted_iota(jnp.int32, (rows, rows), 1)
        allowed = column_ids <= row_ids
        for head in head_list:
            score = jnp.where(allowed, scores_of(head, keys), NEG_BIG)
            top = jnp.max(score, axis=1, keepdims=True)
            weights = jnp.exp2(score - top).astype(jnp.bfloat16)
            top_ref[head] = jnp.broadcast_to(top, (rows, HEAD_WIDTH))
            acc_ref[head] = jnp.dot(weights, values, preferred_element_type=jnp.float32)

    def attend(kv, allowed, last):
        keys, values = kv[:, :HEAD_WIDTH], values_of(kv)
        for head in range(heads):
            score = scores_of(head, keys)
            if allowed is not None:
                score = jnp.where(allowed, score, NEG_BIG)
            old = top_ref[head][:, :1]
            top = jnp.maximum(old, jnp.max(score, axis=1, keepdims=True))
            weights = jnp.exp2(score - top).astype(jnp.bfloat16)
            total = acc_ref[head] * jnp.exp2(old - top) + jnp.dot(
                weights, values, preferred_element_type=jnp.float32
            )
            if last:
                out_ref[:, head * HEAD_WIDTH : (head + 1) * HEAD_WIDTH] = (
                    total[:, :HEAD_WIDTH] / total[:, HEAD_WIDTH:]
                ).astype(out_ref.dtype)
            else:
                top_ref[head] = jnp.broadcast_to(top, (rows, HEAD_WIDTH))
                acc_ref[head] = total

    query_in.wait()
    first_attend(range(heads // 2))

    hidden_in.wait()
    partial = None
    for cut in range(WEIGHT_CUTS):
        weight_in[cut].wait()
        span = slice(cut * depth, (cut + 1) * depth)
        product = jnp.dot(
            hidden_ref[:, span], weight_ref[span, :], preferred_element_type=jnp.float32
        )
        partial = product if partial is None else partial + product
    down_in.wait()
    up_in.wait()
    adapters, rank_width, width = down_ref.shape
    delta = lax.dot_general(
        hidden_ref[...],
        down_ref[...].reshape(adapters * rank_width, width),
        (((1,), (1,)), ((), ())),
        preferred_element_type=jnp.float32,
    )
    adapter_of = lax.broadcasted_iota(jnp.int32, delta.shape, 1) // rank_width
    delta = jnp.where(adapter_of == adapter_ref[0], delta, 0.0)
    up_all = up_ref[...].reshape(adapters * rank_width, up_ref.shape[2]).astype(jnp.float32)
    part_send[...] = partial + ADAPTER_SCALE * jnp.dot(
        delta, up_all, preferred_element_type=jnp.float32, precision=lax.Precision.HIGHEST
    )
    part_copy = pltpu.make_async_remote_copy(
        src_ref=part_send,
        dst_ref=part_recv,
        send_sem=part_sem.at[0],
        recv_sem=part_sem.at[1],
        device_id={"rep": partner},
        device_id_type=MESH,
    )
    part_copy.start()

    @pl.when(me > 0)
    def _():
        take_token(0)

    first_attend(range(heads // 2, heads))

    part_copy.wait_recv()
    present = lax.broadcasted_iota(jnp.int32, part_send.shape, 0) // BLOCK < count_ref[me]
    rebuilt_ref[...] = jnp.where(present, part_send[...] + part_recv[...], 0.0).astype(
        jnp.bfloat16
    )
    miss_all[me] = rebuilt_ref[:, columns]
    for step in range(1, pool_size):
        target = lax.rem(me + step, pool_size)
        remote(miss_all, me, target, miss_send, miss_recv).start()

    @pl.when(me > 1)
    def _():
        take_token(1)

    def earlier(step, carry):
        @pl.when(step > 1)
        def _():
            take_token(step)

        attend(token_all[me - 1 - step], None, False)
        return carry

    lax.fori_loop(0, me, earlier, 0)

    for step in range(1, pool_size):
        source = lax.rem(me + step, pool_size)
        remote(hit_all, source, source, hit_send, hit_recv).wait_recv()
    for i in range(hits):
        extra_kv[i * BLOCK : (i + 1) * BLOCK, :] = hit_all[
            jnp.clip(owners[i], 0, pool_size - 1), jnp.minimum(ranks[i], OWNER_MOST - 1)
        ]
    for step in range(1, pool_size):
        source = lax.rem(me + step, pool_size)
        remote(miss_all, source, source, miss_send, miss_recv).wait_recv()
    for holder in range(pool_size):
        start = hits * BLOCK + holder * miss_rows
        extra_kv[start : start + miss_rows, :] = miss_all[holder]

    extra_rows = extra_kv.shape[0]
    ids = lax.broadcasted_iota(jnp.int32, (1, extra_rows), 1) - hits * BLOCK
    live = jnp.where(ids < 0, 1, 0)
    for holder in range(pool_size):
        offset = ids - holder * miss_rows
        limit = jnp.minimum(count_ref[holder], miss_slots) * BLOCK
        live = live + jnp.where((offset >= 0) & (offset < limit), 1, 0)
    attend(extra_kv[...], live > 0, True)

    for source in range(pool_size):

        @pl.when((source <= me) & (me + 1 < pool_size))
        def _():
            token_copy(source).wait_send()

    for step in range(1, pool_size):
        target = lax.rem(me + step, pool_size)
        remote(hit_all, me, target, hit_send, hit_recv).wait_send()
        remote(miss_all, me, target, miss_send, miss_recv).wait_send()
    part_copy.wait_send()


def shards(
    queries,
    token_key_value,
    key_value_cache,
    cached_block_slots,
    absent_hidden_rows,
    absent_block_count,
    adapter,
    key_value_weight,
    down_weight_stack,
    up_weight_stack,
):
    pool_size = lax.axis_size("pool")
    rows, query_width = queries.shape
    heads = query_width // HEAD_WIDTH
    slot_count = key_value_cache.shape[0]
    hits = cached_block_slots.shape[0]
    miss_rows = absent_hidden_rows.shape[0]
    kv_columns = token_key_value.shape[1]
    extra_rows = hits * BLOCK + pool_size * miss_rows
    smem = pl.BlockSpec(memory_space=pltpu.SMEM)
    anywhere = pl.BlockSpec(memory_space=pl.ANY)
    vmem = pl.BlockSpec(memory_space=pltpu.VMEM)
    dma = pltpu.SemaphoreType.DMA
    bf16 = jnp.bfloat16
    return pl.pallas_call(
        functools.partial(kernel, pool_size),
        out_shape=(
            jax.ShapeDtypeStruct((rows, query_width), bf16),
            jax.ShapeDtypeStruct((miss_rows, kv_columns), bf16),
        ),
        in_specs=[smem] * 3 + [anywhere] * 7,
        out_specs=(vmem, vmem),
        scratch_shapes=[
            pltpu.VMEM((rows, query_width), bf16),
            pltpu.VMEM((pool_size, rows, KV_WIDTH), bf16),
            pltpu.VMEM((slot_count, BLOCK, KV_WIDTH), bf16),
            pltpu.VMEM(absent_hidden_rows.shape, bf16),
            pltpu.VMEM(key_value_weight.shape, bf16),
            pltpu.VMEM(down_weight_stack.shape, bf16),
            pltpu.VMEM(up_weight_stack.shape, bf16),
            pltpu.VMEM((pool_size, OWNER_MOST, BLOCK, KV_WIDTH), bf16),
            pltpu.VMEM((pool_size, miss_rows, KV_WIDTH), bf16),
            pltpu.VMEM((miss_rows, kv_columns), jnp.float32),
            pltpu.VMEM((miss_rows, kv_columns), jnp.float32),
            pltpu.VMEM((extra_rows, KV_WIDTH), bf16),
            pltpu.VMEM((heads, rows, HEAD_WIDTH), jnp.float32),
            pltpu.VMEM((heads, rows, KV_WIDTH), jnp.float32),
            dma((6,)),
            dma((WEIGHT_CUTS,)),
            dma((pool_size,)),
            dma((pool_size,)),
            dma((pool_size,)),
            dma((pool_size,)),
            dma((pool_size,)),
            dma((pool_size,)),
            dma((2,)),
        ],
        compiler_params=pltpu.CompilerParams(
            collective_id=0, has_side_effects=True, vmem_limit_bytes=63 * 1024 * 1024
        ),
        cost_estimate=pl.CostEstimate(
            flops=4 * heads * rows * HEAD_WIDTH * (pool_size * rows + extra_rows),
            bytes_accessed=key_value_weight.size * 2,
            transcendentals=heads * rows * (pool_size * rows + extra_rows),
        ),
    )(
        cached_block_slots,
        absent_block_count,
        adapter,
        queries,
        token_key_value,
        key_value_cache,
        absent_hidden_rows,
        key_value_weight,
        down_weight_stack,
        up_weight_stack,
    )


def solution(mesh):
    in_specs = (
        P(("groups", "pool"), ("head", "rep")),
        P(("groups", "pool"), "head"),
        P(("groups", "pool"), None, "head"),
        P("groups"),
        P(("groups", "pool"), "rep"),
        P("groups"),
        P("groups"),
        P("rep", "head"),
        P(None, None, "rep"),
        P(None, None, "head"),
    )
    out_specs = (P(("groups", "pool"), ("head", "rep")), P(("groups", "pool"), "head"))
    return jax.shard_map(shards, mesh=mesh, in_specs=in_specs, out_specs=out_specs, check_vma=False)
```

```python
import functools
import math

import jax
import jax.numpy as jnp
from jax import lax
from jax.experimental import pallas as pl
from jax.experimental.pallas import tpu as pltpu
from jax.sharding import PartitionSpec as P

HEAD_WIDTH = 128
KV_WIDTH = 2 * HEAD_WIDTH
KV_GROUP = 8
BLOCK = 16
ADAPTER_SCALE = 2.0
NEG_BIG = -1e30
MESH = pl.DeviceIdType.MESH
SCORE_SCALE = HEAD_WIDTH ** -0.5 * math.log2(math.e)
WEIGHT_CUTS = 4


def kernel(
    pool_size,
    slots_ref,
    count_ref,
    adapter_ref,
    query_hbm,
    token_hbm,
    cache_hbm,
    hidden_hbm,
    weight_hbm,
    down_hbm,
    up_hbm,
    out_ref,
    rebuilt_ref,
    query_ref,
    token_all,
    cache_ref,
    hidden_ref,
    weight_ref,
    down_ref,
    up_ref,
    up_hits,
    up_out,
    down_hits,
    down_out,
    miss_all,
    part_send,
    part_recv,
    extra_kv,
    top_ref,
    acc_ref,
    local_sem,
    weight_sem,
    token_send,
    token_recv,
    hit_send,
    hit_recv,
    miss_send,
    miss_recv,
    part_sem,
):
    me = lax.axis_index("pool")
    core = lax.axis_index("rep")
    partner = 1 - core
    hits = slots_ref.shape[0]
    slot_count = cache_ref.shape[0]
    rows = query_ref.shape[0]
    heads = query_ref.shape[1] // HEAD_WIDTH
    first_head = core * heads // KV_GROUP
    columns = pl.ds(pl.multiple_of(first_head * KV_WIDTH, KV_WIDTH), KV_WIDTH)
    miss_rows = hidden_ref.shape[0]
    miss_slots = miss_rows // BLOCK

    barrier = pltpu.get_barrier_semaphore()
    for step in range(1, pool_size):
        pl.semaphore_signal(
            barrier, inc=1, device_id={"pool": lax.rem(me + step, pool_size)}, device_id_type=MESH
        )
    pl.semaphore_signal(barrier, inc=1, device_id={"rep": partner}, device_id_type=MESH)

    token_in = pltpu.make_async_copy(token_hbm.at[:, columns], token_all.at[me], local_sem.at[0])
    cache_in = pltpu.make_async_copy(cache_hbm.at[:, :, columns], cache_ref, local_sem.at[1])
    query_in = pltpu.make_async_copy(query_hbm, query_ref, local_sem.at[2])
    hidden_in = pltpu.make_async_copy(hidden_hbm, hidden_ref, local_sem.at[3])
    down_in = pltpu.make_async_copy(down_hbm, down_ref, local_sem.at[4])
    up_in = pltpu.make_async_copy(up_hbm, up_ref, local_sem.at[5])
    token_in.start()
    cache_in.start()
    query_in.start()
    hidden_in.start()
    depth = weight_ref.shape[0] // WEIGHT_CUTS
    weight_in = []
    for cut in range(WEIGHT_CUTS):
        span = pl.ds(cut * depth, depth)
        copy = pltpu.make_async_copy(weight_hbm.at[span], weight_ref.at[span], weight_sem.at[cut])
        copy.start()
        weight_in.append(copy)
    down_in.start()
    up_in.start()

    slot_ids = [slots_ref[i] for i in range(hits)]
    owners = [slot // slot_count for slot in slot_ids]
    cache_in.wait()

    def own_block(i):
        return cache_ref[lax.rem(slot_ids[i], slot_count)]

    def up_copy():
        return pltpu.make_async_remote_copy(
            src_ref=up_out,
            dst_ref=up_hits,
            send_sem=hit_send.at[0],
            recv_sem=hit_recv.at[0],
            device_id={"pool": lax.rem(me + 1, pool_size)},
            device_id_type=MESH,
        )

    def down_copy():
        return pltpu.make_async_remote_copy(
            src_ref=down_out,
            dst_ref=down_hits,
            send_sem=hit_send.at[1],
            recv_sem=hit_recv.at[1],
            device_id={"pool": lax.rem(me + pool_size - 1, pool_size)},
            device_id_type=MESH,
        )

    def pass_hits(hop):
        @pl.when(me == hop)
        def _():
            up_copy().wait_recv()
            for i in range(hits):
                up_out[i] = jnp.where(owners[i] == me, own_block(i), up_hits[i])
            up_copy().start()

        @pl.when(pool_size - 1 - me == hop)
        def _():
            down_copy().wait_recv()
            for i in range(hits):
                down_out[i] = jnp.where(owners[i] == me, own_block(i), down_hits[i])
            down_copy().start()

    for i in range(hits):
        extra_kv[i * BLOCK : (i + 1) * BLOCK, :] = own_block(i)

    @pl.when(me == 0)
    def _():
        for i in range(hits):
            up_out[i] = own_block(i)

    @pl.when(me == pool_size - 1)
    def _():
        for i in range(hits):
            down_out[i] = own_block(i)

    token_in.wait()

    def remote(buffer, source, target, send, receive):
        return pltpu.make_async_remote_copy(
            src_ref=buffer.at[source],
            dst_ref=buffer.at[source],
            send_sem=send.at[target],
            recv_sem=receive.at[source],
            device_id={"pool": target},
            device_id_type=MESH,
        )

    pl.semaphore_wait(barrier, pool_size)

    def token_copy(source):
        return pltpu.make_async_remote_copy(
            src_ref=token_all.at[source],
            dst_ref=token_all.at[source],
            send_sem=token_send.at[source],
            recv_sem=token_recv.at[source],
            device_id={"pool": lax.rem(me + 1, pool_size)},
            device_id_type=MESH,
        )

    def take_token(step):
        token_copy(me - 1 - step).wait_recv()

        @pl.when(me + 1 < pool_size)
        def _():
            token_copy(me - 1 - step).start()

    @pl.when(me + 1 < pool_size)
    def _():
        token_copy(me).start()

    @pl.when(me == 0)
    def _():
        up_copy().start()

    @pl.when(me == pool_size - 1)
    def _():
        down_copy().start()

    def scores_of(head, keys):
        query = query_ref[:, head * HEAD_WIDTH : (head + 1) * HEAD_WIDTH]
        return (
            lax.dot_general(
                query, keys, (((1,), (1,)), ((), ())), preferred_element_type=jnp.float32
            )
            * SCORE_SCALE
        )

    def values_of(kv):
        return jnp.concatenate(
            [kv[:, HEAD_WIDTH:], jnp.ones((kv.shape[0], HEAD_WIDTH), kv.dtype)], axis=1
        )

    def first_attend(head_list):
        kv = token_all[me]
        keys, values = kv[:, :HEAD_WIDTH], values_of(kv)
        row_ids = lax.broadcasted_iota(jnp.int32, (rows, rows), 0)
        column_ids = lax.broadcasted_iota(jnp.int32, (rows, rows), 1)
        allowed = column_ids <= row_ids
        for head in head_list:
            score = jnp.where(allowed, scores_of(head, keys), NEG_BIG)
            top = jnp.max(score, axis=1, keepdims=True)
            weights = jnp.exp2(score - top).astype(jnp.bfloat16)
            top_ref[head] = jnp.broadcast_to(top, (rows, HEAD_WIDTH))
            acc_ref[head] = jnp.dot(weights, values, preferred_element_type=jnp.float32)

    def attend(kv, allowed, last):
        keys, values = kv[:, :HEAD_WIDTH], values_of(kv)
        for head in range(heads):
            score = scores_of(head, keys)
            if allowed is not None:
                score = jnp.where(allowed, score, NEG_BIG)
            old = top_ref[head][:, :1]
            top = jnp.maximum(old, jnp.max(score, axis=1, keepdims=True))
            weights = jnp.exp2(score - top).astype(jnp.bfloat16)
            total = acc_ref[head] * jnp.exp2(old - top) + jnp.dot(
                weights, values, preferred_element_type=jnp.float32
            )
            if last:
                out_ref[:, head * HEAD_WIDTH : (head + 1) * HEAD_WIDTH] = (
                    total[:, :HEAD_WIDTH] / total[:, HEAD_WIDTH:]
                ).astype(out_ref.dtype)
            else:
                top_ref[head] = jnp.broadcast_to(top, (rows, HEAD_WIDTH))
                acc_ref[head] = total

    first_heads = heads * 3 // 4
    query_in.wait()
    first_attend(range(first_heads))

    @pl.when(me > 0)
    def _():
        take_token(0)

    pass_hits(1)

    hidden_in.wait()
    partial = None
    for cut in range(WEIGHT_CUTS):
        weight_in[cut].wait()
        span = slice(cut * depth, (cut + 1) * depth)
        product = jnp.dot(
            hidden_ref[:, span], weight_ref[span, :], preferred_element_type=jnp.float32
        )
        partial = product if partial is None else partial + product
    down_in.wait()
    up_in.wait()
    adapters, rank_width, width = down_ref.shape
    delta = lax.dot_general(
        hidden_ref[...],
        down_ref[...].reshape(adapters * rank_width, width),
        (((1,), (1,)), ((), ())),
        preferred_element_type=jnp.float32,
    )
    adapter_of = lax.broadcasted_iota(jnp.int32, delta.shape, 1) // rank_width
    delta = jnp.where(adapter_of == adapter_ref[0], delta, 0.0)
    up_all = up_ref[...].reshape(adapters * rank_width, up_ref.shape[2]).astype(jnp.float32)
    part_send[...] = partial + ADAPTER_SCALE * jnp.dot(
        delta, up_all, preferred_element_type=jnp.float32, precision=lax.Precision.HIGHEST
    )
    part_copy = pltpu.make_async_remote_copy(
        src_ref=part_send,
        dst_ref=part_recv,
        send_sem=part_sem.at[0],
        recv_sem=part_sem.at[1],
        device_id={"rep": partner},
        device_id_type=MESH,
    )
    part_copy.start()

    @pl.when(me > 1)
    def _():
        take_token(1)

    pass_hits(2)
    first_attend(range(first_heads, heads))

    part_copy.wait_recv()
    present = lax.broadcasted_iota(jnp.int32, part_send.shape, 0) // BLOCK < count_ref[me]
    rebuilt_ref[...] = jnp.where(present, part_send[...] + part_recv[...], 0.0).astype(
        jnp.bfloat16
    )
    miss_all[me] = rebuilt_ref[:, columns]
    for step in range(1, pool_size):
        target = lax.rem(me + step, pool_size)
        remote(miss_all, me, target, miss_send, miss_recv).start()

    def earlier(step, carry):
        @pl.when(step > 1)
        def _():
            take_token(step)

        attend(token_all[me - 1 - step], None, False)
        return carry

    lax.fori_loop(0, me, earlier, 0)

    for hop in range(3, pool_size - 1):
        pass_hits(hop)

    @pl.when(me == pool_size - 1)
    def _():
        up_copy().wait_recv()

    @pl.when(me == 0)
    def _():
        down_copy().wait_recv()

    @pl.when(me > 0)
    def _():
        for i in range(hits):
            span = slice(i * BLOCK, (i + 1) * BLOCK)
            extra_kv[span, :] = jnp.where(owners[i] < me, up_hits[i], extra_kv[span, :])

    @pl.when(me < pool_size - 1)
    def _():
        for i in range(hits):
            span = slice(i * BLOCK, (i + 1) * BLOCK)
            extra_kv[span, :] = jnp.where(owners[i] > me, down_hits[i], extra_kv[span, :])

    for step in range(1, pool_size):
        source = lax.rem(me + step, pool_size)
        remote(miss_all, source, source, miss_send, miss_recv).wait_recv()
    for holder in range(pool_size):
        start = hits * BLOCK + holder * miss_rows
        extra_kv[start : start + miss_rows, :] = miss_all[holder]

    extra_rows = extra_kv.shape[0]
    ids = lax.broadcasted_iota(jnp.int32, (1, extra_rows), 1) - hits * BLOCK
    live = jnp.where(ids < 0, 1, 0)
    for holder in range(pool_size):
        offset = ids - holder * miss_rows
        limit = jnp.minimum(count_ref[holder], miss_slots) * BLOCK
        live = live + jnp.where((offset >= 0) & (offset < limit), 1, 0)
    attend(extra_kv[...], live > 0, True)

    for source in range(pool_size):

        @pl.when((source <= me) & (me + 1 < pool_size))
        def _():
            token_copy(source).wait_send()

    for step in range(1, pool_size):
        target = lax.rem(me + step, pool_size)
        remote(miss_all, me, target, miss_send, miss_recv).wait_send()
    part_copy.wait_send()

    @pl.when(me < pool_size - 1)
    def _():
        up_copy().wait_send()

    @pl.when(me > 0)
    def _():
        down_copy().wait_send()


def shards(
    queries,
    token_key_value,
    key_value_cache,
    cached_block_slots,
    absent_hidden_rows,
    absent_block_count,
    adapter,
    key_value_weight,
    down_weight_stack,
    up_weight_stack,
):
    pool_size = lax.axis_size("pool")
    rows, query_width = queries.shape
    heads = query_width // HEAD_WIDTH
    slot_count = key_value_cache.shape[0]
    hits = cached_block_slots.shape[0]
    miss_rows = absent_hidden_rows.shape[0]
    kv_columns = token_key_value.shape[1]
    extra_rows = hits * BLOCK + pool_size * miss_rows
    smem = pl.BlockSpec(memory_space=pltpu.SMEM)
    anywhere = pl.BlockSpec(memory_space=pl.ANY)
    vmem = pl.BlockSpec(memory_space=pltpu.VMEM)
    dma = pltpu.SemaphoreType.DMA
    bf16 = jnp.bfloat16
    return pl.pallas_call(
        functools.partial(kernel, pool_size),
        out_shape=(
            jax.ShapeDtypeStruct((rows, query_width), bf16),
            jax.ShapeDtypeStruct((miss_rows, kv_columns), bf16),
        ),
        in_specs=[smem] * 3 + [anywhere] * 7,
        out_specs=(vmem, vmem),
        scratch_shapes=[
            pltpu.VMEM((rows, query_width), bf16),
            pltpu.VMEM((pool_size, rows, KV_WIDTH), bf16),
            pltpu.VMEM((slot_count, BLOCK, KV_WIDTH), bf16),
            pltpu.VMEM(absent_hidden_rows.shape, bf16),
            pltpu.VMEM(key_value_weight.shape, bf16),
            pltpu.VMEM(down_weight_stack.shape, bf16),
            pltpu.VMEM(up_weight_stack.shape, bf16),
            pltpu.VMEM((hits, BLOCK, KV_WIDTH), bf16),
            pltpu.VMEM((hits, BLOCK, KV_WIDTH), bf16),
            pltpu.VMEM((hits, BLOCK, KV_WIDTH), bf16),
            pltpu.VMEM((hits, BLOCK, KV_WIDTH), bf16),
            pltpu.VMEM((pool_size, miss_rows, KV_WIDTH), bf16),
            pltpu.VMEM((miss_rows, kv_columns), jnp.float32),
            pltpu.VMEM((miss_rows, kv_columns), jnp.float32),
            pltpu.VMEM((extra_rows, KV_WIDTH), bf16),
            pltpu.VMEM((heads, rows, HEAD_WIDTH), jnp.float32),
            pltpu.VMEM((heads, rows, KV_WIDTH), jnp.float32),
            dma((6,)),
            dma((WEIGHT_CUTS,)),
            dma((pool_size,)),
            dma((pool_size,)),
            dma((2,)),
            dma((2,)),
            dma((pool_size,)),
            dma((pool_size,)),
            dma((2,)),
        ],
        compiler_params=pltpu.CompilerParams(
            collective_id=0, has_side_effects=True, vmem_limit_bytes=63 * 1024 * 1024
        ),
        cost_estimate=pl.CostEstimate(
            flops=4 * heads * rows * HEAD_WIDTH * (pool_size * rows + extra_rows),
            bytes_accessed=key_value_weight.size * 2,
            transcendentals=heads * rows * (pool_size * rows + extra_rows),
        ),
    )(
        cached_block_slots,
        absent_block_count,
        adapter,
        queries,
        token_key_value,
        key_value_cache,
        absent_hidden_rows,
        key_value_weight,
        down_weight_stack,
        up_weight_stack,
    )


def solution(mesh):
    in_specs = (
        P(("groups", "pool"), ("head", "rep")),
        P(("groups", "pool"), "head"),
        P(("groups", "pool"), None, "head"),
        P("groups"),
        P(("groups", "pool"), "rep"),
        P("groups"),
        P("groups"),
        P("rep", "head"),
        P(None, None, "rep"),
        P(None, None, "head"),
    )
    out_specs = (P(("groups", "pool"), ("head", "rep")), P(("groups", "pool"), "head"))
    return jax.shard_map(shards, mesh=mesh, in_specs=in_specs, out_specs=out_specs, check_vma=False)
```

```python
import functools
import math

import jax
import jax.numpy as jnp
from jax import lax
from jax.experimental import pallas as pl
from jax.experimental.pallas import tpu as pltpu
from jax.sharding import PartitionSpec as P

HEAD_WIDTH = 128
KV_WIDTH = 2 * HEAD_WIDTH
KV_GROUP = 8
BLOCK = 16
ADAPTER_SCALE = 2.0
NEG_BIG = -1e30
MESH = pl.DeviceIdType.MESH
SCORE_SCALE = HEAD_WIDTH ** -0.5 * math.log2(math.e)
WEIGHT_CUTS = 4


def kernel(
    pool_size,
    slots_ref,
    count_ref,
    adapter_ref,
    query_hbm,
    token_hbm,
    cache_hbm,
    hidden_hbm,
    weight_hbm,
    down_hbm,
    up_hbm,
    out_ref,
    rebuilt_ref,
    query_ref,
    token_all,
    cache_ref,
    hidden_ref,
    weight_ref,
    down_ref,
    up_ref,
    up_hits,
    up_out,
    down_hits,
    down_out,
    miss_all,
    part_send,
    part_recv,
    extra_kv,
    top_ref,
    acc_ref,
    local_sem,
    weight_sem,
    token_send,
    token_recv,
    hit_send,
    hit_recv,
    miss_send,
    miss_recv,
    part_sem,
):
    me = lax.axis_index("pool")
    core = lax.axis_index("rep")
    partner = 1 - core
    hits = slots_ref.shape[0]
    slot_count = cache_ref.shape[0]
    rows = query_ref.shape[0]
    heads = query_ref.shape[1] // HEAD_WIDTH
    first_head = core * heads // KV_GROUP
    columns = pl.ds(pl.multiple_of(first_head * KV_WIDTH, KV_WIDTH), KV_WIDTH)
    miss_rows = hidden_ref.shape[0]
    miss_slots = miss_rows // BLOCK

    barrier = pltpu.get_barrier_semaphore()
    for step in range(1, pool_size):
        pl.semaphore_signal(
            barrier, inc=1, device_id={"pool": lax.rem(me + step, pool_size)}, device_id_type=MESH
        )
    pl.semaphore_signal(barrier, inc=1, device_id={"rep": partner}, device_id_type=MESH)

    token_in = pltpu.make_async_copy(token_hbm.at[:, columns], token_all.at[me], local_sem.at[0])
    cache_in = pltpu.make_async_copy(cache_hbm.at[:, :, columns], cache_ref, local_sem.at[1])
    query_in = pltpu.make_async_copy(query_hbm, query_ref, local_sem.at[2])
    hidden_in = pltpu.make_async_copy(hidden_hbm, hidden_ref, local_sem.at[3])
    down_in = pltpu.make_async_copy(down_hbm, down_ref, local_sem.at[4])
    up_in = pltpu.make_async_copy(up_hbm, up_ref, local_sem.at[5])
    token_in.start()
    cache_in.start()
    query_in.start()
    hidden_in.start()
    depth = weight_ref.shape[0] // WEIGHT_CUTS
    weight_in = []
    for cut in range(WEIGHT_CUTS):
        span = pl.ds(cut * depth, depth)
        copy = pltpu.make_async_copy(weight_hbm.at[span], weight_ref.at[span], weight_sem.at[cut])
        copy.start()
        weight_in.append(copy)
    down_in.start()
    up_in.start()

    slot_ids = [slots_ref[i] for i in range(hits)]
    owners = [slot // slot_count for slot in slot_ids]
    cache_in.wait()

    def own_block(i):
        return cache_ref[lax.rem(slot_ids[i], slot_count)]

    def up_copy():
        return pltpu.make_async_remote_copy(
            src_ref=up_out,
            dst_ref=up_hits,
            send_sem=hit_send.at[0],
            recv_sem=hit_recv.at[0],
            device_id={"pool": lax.rem(me + 1, pool_size)},
            device_id_type=MESH,
        )

    def down_copy():
        return pltpu.make_async_remote_copy(
            src_ref=down_out,
            dst_ref=down_hits,
            send_sem=hit_send.at[1],
            recv_sem=hit_recv.at[1],
            device_id={"pool": lax.rem(me + pool_size - 1, pool_size)},
            device_id_type=MESH,
        )

    def pass_hits(hop):
        @pl.when(me == hop)
        def _():
            up_copy().wait_recv()
            for i in range(hits):
                up_out[i] = jnp.where(owners[i] == me, own_block(i), up_hits[i])
            up_copy().start()

        @pl.when(pool_size - 1 - me == hop)
        def _():
            down_copy().wait_recv()
            for i in range(hits):
                down_out[i] = jnp.where(owners[i] == me, own_block(i), down_hits[i])
            down_copy().start()

    for i in range(hits):
        extra_kv[i * BLOCK : (i + 1) * BLOCK, :] = own_block(i)

    @pl.when(me == 0)
    def _():
        for i in range(hits):
            up_out[i] = own_block(i)

    @pl.when(me == pool_size - 1)
    def _():
        for i in range(hits):
            down_out[i] = own_block(i)

    token_in.wait()

    def remote(buffer, source, target, send, receive):
        return pltpu.make_async_remote_copy(
            src_ref=buffer.at[source],
            dst_ref=buffer.at[source],
            send_sem=send.at[target],
            recv_sem=receive.at[source],
            device_id={"pool": target},
            device_id_type=MESH,
        )

    pl.semaphore_wait(barrier, pool_size)

    def token_copy(source):
        return pltpu.make_async_remote_copy(
            src_ref=token_all.at[source],
            dst_ref=token_all.at[source],
            send_sem=token_send.at[source],
            recv_sem=token_recv.at[source],
            device_id={"pool": lax.rem(me + 1, pool_size)},
            device_id_type=MESH,
        )

    def take_token(step):
        token_copy(me - 1 - step).wait_recv()

        @pl.when(me + 1 < pool_size)
        def _():
            token_copy(me - 1 - step).start()

    @pl.when(me + 1 < pool_size)
    def _():
        token_copy(me).start()

    @pl.when(me == 0)
    def _():
        up_copy().start()

    @pl.when(me == pool_size - 1)
    def _():
        down_copy().start()

    def scores_of(head, keys):
        query = query_ref[:, head * HEAD_WIDTH : (head + 1) * HEAD_WIDTH]
        return (
            lax.dot_general(
                query, keys, (((1,), (1,)), ((), ())), preferred_element_type=jnp.float32
            )
            * SCORE_SCALE
        )

    def values_of(kv):
        return jnp.concatenate(
            [kv[:, HEAD_WIDTH:], jnp.ones((kv.shape[0], HEAD_WIDTH), kv.dtype)], axis=1
        )

    def first_attend(head_list):
        kv = token_all[me]
        keys, values = kv[:, :HEAD_WIDTH], values_of(kv)
        row_ids = lax.broadcasted_iota(jnp.int32, (rows, rows), 0)
        column_ids = lax.broadcasted_iota(jnp.int32, (rows, rows), 1)
        allowed = column_ids <= row_ids
        for head in head_list:
            score = jnp.where(allowed, scores_of(head, keys), NEG_BIG)
            top = jnp.max(score, axis=1, keepdims=True)
            weights = jnp.exp2(score - top).astype(jnp.bfloat16)
            top_ref[head] = jnp.broadcast_to(top, (rows, HEAD_WIDTH))
            acc_ref[head] = jnp.dot(weights, values, preferred_element_type=jnp.float32)

    def attend(kv, allowed, last):
        keys, values = kv[:, :HEAD_WIDTH], values_of(kv)
        for head in range(heads):
            score = scores_of(head, keys)
            if allowed is not None:
                score = jnp.where(allowed, score, NEG_BIG)
            old = top_ref[head][:, :1]
            top = jnp.maximum(old, jnp.max(score, axis=1, keepdims=True))
            weights = jnp.exp2(score - top).astype(jnp.bfloat16)
            total = acc_ref[head] * jnp.exp2(old - top) + jnp.dot(
                weights, values, preferred_element_type=jnp.float32
            )
            if last:
                out_ref[:, head * HEAD_WIDTH : (head + 1) * HEAD_WIDTH] = (
                    total[:, :HEAD_WIDTH] / total[:, HEAD_WIDTH:]
                ).astype(out_ref.dtype)
            else:
                top_ref[head] = jnp.broadcast_to(top, (rows, HEAD_WIDTH))
                acc_ref[head] = total

    first_heads = heads * 3 // 4
    query_in.wait()

    hidden_in.wait()
    partial = None
    for cut in range(WEIGHT_CUTS):
        weight_in[cut].wait()
        span = slice(cut * depth, (cut + 1) * depth)
        product = jnp.dot(
            hidden_ref[:, span], weight_ref[span, :], preferred_element_type=jnp.float32
        )
        partial = product if partial is None else partial + product
    down_in.wait()
    up_in.wait()
    adapters, rank_width, width = down_ref.shape
    delta = lax.dot_general(
        hidden_ref[...],
        down_ref[...].reshape(adapters * rank_width, width),
        (((1,), (1,)), ((), ())),
        preferred_element_type=jnp.float32,
    )
    adapter_of = lax.broadcasted_iota(jnp.int32, delta.shape, 1) // rank_width
    delta = jnp.where(adapter_of == adapter_ref[0], delta, 0.0)
    up_all = up_ref[...].reshape(adapters * rank_width, up_ref.shape[2]).astype(jnp.float32)
    part_send[...] = partial + ADAPTER_SCALE * jnp.dot(
        delta, up_all, preferred_element_type=jnp.float32, precision=lax.Precision.HIGHEST
    )
    part_copy = pltpu.make_async_remote_copy(
        src_ref=part_send,
        dst_ref=part_recv,
        send_sem=part_sem.at[0],
        recv_sem=part_sem.at[1],
        device_id={"rep": partner},
        device_id_type=MESH,
    )
    part_copy.start()
    first_attend(range(first_heads))
    first_attend(range(first_heads, heads))

    part_copy.wait_recv()
    present = lax.broadcasted_iota(jnp.int32, part_send.shape, 0) // BLOCK < count_ref[me]
    rebuilt_ref[...] = jnp.where(present, part_send[...] + part_recv[...], 0.0).astype(
        jnp.bfloat16
    )
    miss_all[me] = rebuilt_ref[:, columns]
    for step in range(1, pool_size):
        target = lax.rem(me + step, pool_size)
        remote(miss_all, me, target, miss_send, miss_recv).start()

    @pl.when(me > 0)
    def _():
        take_token(0)

    pass_hits(1)

    @pl.when(me > 1)
    def _():
        take_token(1)

    pass_hits(2)

    def earlier(step, carry):
        @pl.when(step > 1)
        def _():
            take_token(step)

        attend(token_all[me - 1 - step], None, False)
        return carry

    lax.fori_loop(0, me, earlier, 0)

    for hop in range(3, pool_size - 1):
        pass_hits(hop)

    @pl.when(me == pool_size - 1)
    def _():
        up_copy().wait_recv()

    @pl.when(me == 0)
    def _():
        down_copy().wait_recv()

    @pl.when(me > 0)
    def _():
        for i in range(hits):
            span = slice(i * BLOCK, (i + 1) * BLOCK)
            extra_kv[span, :] = jnp.where(owners[i] < me, up_hits[i], extra_kv[span, :])

    @pl.when(me < pool_size - 1)
    def _():
        for i in range(hits):
            span = slice(i * BLOCK, (i + 1) * BLOCK)
            extra_kv[span, :] = jnp.where(owners[i] > me, down_hits[i], extra_kv[span, :])

    for step in range(1, pool_size):
        source = lax.rem(me + step, pool_size)
        remote(miss_all, source, source, miss_send, miss_recv).wait_recv()
    for holder in range(pool_size):
        start = hits * BLOCK + holder * miss_rows
        extra_kv[start : start + miss_rows, :] = miss_all[holder]

    extra_rows = extra_kv.shape[0]
    ids = lax.broadcasted_iota(jnp.int32, (1, extra_rows), 1) - hits * BLOCK
    live = jnp.where(ids < 0, 1, 0)
    for holder in range(pool_size):
        offset = ids - holder * miss_rows
        limit = jnp.minimum(count_ref[holder], miss_slots) * BLOCK
        live = live + jnp.where((offset >= 0) & (offset < limit), 1, 0)
    attend(extra_kv[...], live > 0, True)

    for source in range(pool_size):

        @pl.when((source <= me) & (me + 1 < pool_size))
        def _():
            token_copy(source).wait_send()

    for step in range(1, pool_size):
        target = lax.rem(me + step, pool_size)
        remote(miss_all, me, target, miss_send, miss_recv).wait_send()
    part_copy.wait_send()

    @pl.when(me < pool_size - 1)
    def _():
        up_copy().wait_send()

    @pl.when(me > 0)
    def _():
        down_copy().wait_send()


def shards(
    queries,
    token_key_value,
    key_value_cache,
    cached_block_slots,
    absent_hidden_rows,
    absent_block_count,
    adapter,
    key_value_weight,
    down_weight_stack,
    up_weight_stack,
):
    pool_size = lax.axis_size("pool")
    rows, query_width = queries.shape
    heads = query_width // HEAD_WIDTH
    slot_count = key_value_cache.shape[0]
    hits = cached_block_slots.shape[0]
    miss_rows = absent_hidden_rows.shape[0]
    kv_columns = token_key_value.shape[1]
    extra_rows = hits * BLOCK + pool_size * miss_rows
    smem = pl.BlockSpec(memory_space=pltpu.SMEM)
    anywhere = pl.BlockSpec(memory_space=pl.ANY)
    vmem = pl.BlockSpec(memory_space=pltpu.VMEM)
    dma = pltpu.SemaphoreType.DMA
    bf16 = jnp.bfloat16
    return pl.pallas_call(
        functools.partial(kernel, pool_size),
        out_shape=(
            jax.ShapeDtypeStruct((rows, query_width), bf16),
            jax.ShapeDtypeStruct((miss_rows, kv_columns), bf16),
        ),
        in_specs=[smem] * 3 + [anywhere] * 7,
        out_specs=(vmem, vmem),
        scratch_shapes=[
            pltpu.VMEM((rows, query_width), bf16),
            pltpu.VMEM((pool_size, rows, KV_WIDTH), bf16),
            pltpu.VMEM((slot_count, BLOCK, KV_WIDTH), bf16),
            pltpu.VMEM(absent_hidden_rows.shape, bf16),
            pltpu.VMEM(key_value_weight.shape, bf16),
            pltpu.VMEM(down_weight_stack.shape, bf16),
            pltpu.VMEM(up_weight_stack.shape, bf16),
            pltpu.VMEM((hits, BLOCK, KV_WIDTH), bf16),
            pltpu.VMEM((hits, BLOCK, KV_WIDTH), bf16),
            pltpu.VMEM((hits, BLOCK, KV_WIDTH), bf16),
            pltpu.VMEM((hits, BLOCK, KV_WIDTH), bf16),
            pltpu.VMEM((pool_size, miss_rows, KV_WIDTH), bf16),
            pltpu.VMEM((miss_rows, kv_columns), jnp.float32),
            pltpu.VMEM((miss_rows, kv_columns), jnp.float32),
            pltpu.VMEM((extra_rows, KV_WIDTH), bf16),
            pltpu.VMEM((heads, rows, HEAD_WIDTH), jnp.float32),
            pltpu.VMEM((heads, rows, KV_WIDTH), jnp.float32),
            dma((6,)),
            dma((WEIGHT_CUTS,)),
            dma((pool_size,)),
            dma((pool_size,)),
            dma((2,)),
            dma((2,)),
            dma((pool_size,)),
            dma((pool_size,)),
            dma((2,)),
        ],
        compiler_params=pltpu.CompilerParams(
            collective_id=0, has_side_effects=True, vmem_limit_bytes=63 * 1024 * 1024
        ),
        cost_estimate=pl.CostEstimate(
            flops=4 * heads * rows * HEAD_WIDTH * (pool_size * rows + extra_rows),
            bytes_accessed=key_value_weight.size * 2,
            transcendentals=heads * rows * (pool_size * rows + extra_rows),
        ),
    )(
        cached_block_slots,
        absent_block_count,
        adapter,
        queries,
        token_key_value,
        key_value_cache,
        absent_hidden_rows,
        key_value_weight,
        down_weight_stack,
        up_weight_stack,
    )


def solution(mesh):
    in_specs = (
        P(("groups", "pool"), ("head", "rep")),
        P(("groups", "pool"), "head"),
        P(("groups", "pool"), None, "head"),
        P("groups"),
        P(("groups", "pool"), "rep"),
        P("groups"),
        P("groups"),
        P("rep", "head"),
        P(None, None, "rep"),
        P(None, None, "head"),
    )
    out_specs = (P(("groups", "pool"), ("head", "rep")), P(("groups", "pool"), "head"))
    return jax.shard_map(shards, mesh=mesh, in_specs=in_specs, out_specs=out_specs, check_vma=False)
```
